32 devices in a mesh: expert: 16 (over z, y, x), pair: 2 (over core).
Axes of the slice: x: 2, y: 2, z: 4, core: 2. Of those that a mesh axis runs over, the one named last changes fastest.
Arguments:
- tokens: bfloat16 [4096, 2048], P(('expert', 'pair')), may hold values from -6 to 6
- out_grads: bfloat16 [4096, 2048], P(('expert', 'pair')), may hold values from -60 to 60
- routing: int32 [4096, 8], P(('expert', 'pair')), may hold values from 0 to 15, all different within a row; in each aligned block of 128 rows (0 to 127, 128 to 255, ...) at most 81 rows name the same one
- combine: float32 [4096, 8], P(('expert', 'pair')), may hold values from 0.05 to 0.3
- weights: bfloat16 [2, 16, 768, 2048], P('pair', 'expert'), may hold values from -6 to 6
- momentum: float32 [2, 16, 768, 2048], P('pair', 'expert'), may hold values from -40 to 40
Outputs:
- momentum_out: float32 [2, 16, 768, 2048], P('pair', 'expert')
- rollout_weights: bfloat16 [2, 16, 768, 2048], P(None, 'expert', 'pair')
The draws below stay inside these ranges and needn't reach their ends.
Inputs may be any that keep to these rules, and one draw needn't show every extreme that they name: `routing`: each row names 8 different experts; within the 128 rows of one device no expert is named more than 81 times, and in some device's rows some expert is named exactly 81 times.
All inputs are finite; a program needn't handle non-finite values.
Results may differ from the reference program's by a relative error of at most 0.005.
Values may be sent and summed in bfloat16 or wider, within the bound.
A program may use at most 128 MiB of HBM per device.

```python
import math
import jax
import jax.numpy as jnp
import numpy as np
from jax import lax

D = 2048
FF = 768
TOPK = 8
TOK_DEV = 128
NS_ITERS = 2
EXPERTS = 16
TOKENS = 4096
CAP = 81
N_EXPERT = 16
N_PAIR = 2


def draw_momentum(key, part):
    key_entries = jax.random.fold_in(key, 11)
    key_rows = jax.random.fold_in(key, 12)
    key_columns = jax.random.fold_in(key, 13)
    row_scale = jnp.exp(jax.random.uniform(key_rows, (2, EXPERTS, FF, 1), jnp.float32, -1.15, 1.15))
    column_scale = jnp.exp(jax.random.uniform(key_columns, (2, EXPERTS, 1, D), jnp.float32, -1.15, 1.15))
    entries = jax.random.normal(key_entries, (2, EXPERTS, FF, D), jnp.float32)
    return jnp.clip(entries * row_scale * column_scale, -40.0, 40.0).astype(jnp.float32)


def level_of(key, extent, split, smallest, largest):
    level = 1.0
    for dim, shards_of in split:
        draws = jax.random.uniform(jax.random.fold_in(jax.random.fold_in(key, 6), dim), (shards_of,), jnp.float32, smallest / len(split), largest / len(split))
        level = level * jnp.repeat(jnp.exp(draws), extent[dim] // shards_of).reshape((-1,) + (1,) * (len(extent) - 1 - dim))
    return level


def shared_out(stream_key, own, number, rows, amount, top, reach, lean):
    order = jax.random.permutation(stream_key, amount)
    crowded, ordinary = shares(amount, rows * top, reach, lean, True), shares(amount, rows * top, reach, lean, False)
    places = jnp.arange(amount)

    def named(lengths, turn):
        used = int((lengths > 0).sum())
        fixed = max(1, used // 4)
        passed = fixed + (places - fixed + turn * (used - fixed)) % max(1, amount - fixed)
        return jnp.zeros((amount,), jnp.int32).at[order[jnp.where(places < fixed, places, passed)]].set(jnp.asarray(lengths, jnp.int32))

    lengths = jnp.where(number % 4 == 0, named(crowded, number // 4), named(ordinary, number - number // 4 - 1))
    mixed = jax.random.permutation(jax.random.fold_in(own, 3), amount)
    source_of, taker = mixed[0:amount // 2 * 2:2], mixed[1:amount // 2 * 2:2]
    slack = jnp.minimum(lengths[source_of] - 1, reach - lengths[taker]) // 2
    slack = jnp.where((source_of == order[0]) | (taker == order[0]) | (lengths[taker] == 0), 0, jnp.maximum(slack, 0))
    passed = jax.random.randint(jax.random.fold_in(own, 4), (amount // 2,), 0, 1 << 20) % (slack + 1)
    lengths = lengths.at[source_of].add(-passed).at[taker].add(passed)
    labels = jnp.searchsorted(jnp.cumsum(lengths), jnp.arange(rows * top), side="right").astype(jnp.int32)
    grid = labels.reshape(top, rows).T
    grid = grid[jax.random.permutation(jax.random.fold_in(own, 1), rows)]
    turn = jax.random.randint(jax.random.fold_in(own, 2), (rows, 1), 0, top)
    return jnp.take_along_axis(grid, (jnp.arange(top)[None, :] + turn) % top, axis=1)


def shares(number_of, total, limit, skew, full):
    portions = [(1 << 20) // math.isqrt(rank ** skew) + 1 for rank in range(1, number_of + 1)]
    largest = limit if full else min(limit, max(-(-total // number_of), total * portions[0] // sum(portions)))
    least = 1 if total - largest >= number_of - 1 else 0
    holding, surplus = [largest] + [least] * (number_of - 1), total - largest - least * (number_of - 1)
    while surplus > 0:
        free = [i for i in range(1, number_of) if holding[i] < largest] or [i for i in range(1, number_of) if holding[i] < limit]
        whole, left = sum([portions[i] for i in free]), surplus
        for i in free:
            extra = min(limit - holding[i], max(1, left * portions[i] // whole), surplus)
            holding[i] = holding[i] + extra
            surplus = surplus - extra
    return np.array(holding)


def gaussian(stream_key, dims, scale, bound, split=(), kind=jnp.bfloat16):
    loudness = level_of(stream_key, dims, split, -0.22, 0.18) if split else 1.0
    drawn = jax.random.normal(stream_key, dims, jnp.float32) * scale * loudness
    return jnp.minimum(jnp.maximum(drawn, -bound), bound).astype(kind)


def setup_inputs(seed: int = 0) -> dict:
    key_list = jax.random.split(jax.random.key(seed), 7)
    tokens = gaussian(key_list[0], (TOKENS, D), 1.0, 6.0, ((0, 32),))
    out_grads = gaussian(key_list[1], (TOKENS, D), 10.0, 60.0, ((0, 32),))
    routing_keys = jax.random.split(jax.random.fold_in(key_list[2], 1), TOKENS // TOK_DEV)
    routing_turns = jax.random.permutation(jax.random.fold_in(key_list[2], 3), TOKENS // TOK_DEV)
    routing = jax.vmap(lambda own, number: shared_out(jax.random.fold_in(key_list[2], 2), own, number, TOK_DEV, EXPERTS, TOPK, CAP, 2))(routing_keys, routing_turns).reshape((TOKENS, TOPK))
    combine = jnp.clip(0.05 + 0.25 * jax.random.uniform(key_list[3], (TOKENS, TOPK), jnp.float32) ** level_of(key_list[3], (TOKENS, TOPK), ((0, 32),), -0.2, 0.2), 0.05, 0.3)
    weights = gaussian(key_list[4], (2, EXPERTS, FF, D), 1.0, 6.0, ((0, 2), (1, 16)))
    momentum = draw_momentum(jax.random.fold_in(key_list[6], 71), 0)
    return dict(tokens=tokens, out_grads=out_grads, routing=routing, combine=combine, weights=weights, momentum=momentum)


COEF_A = 3.4445
COEF_B = -4.775
COEF_C = 2.0315
DECAY = 0.9
NORM_EPS = 1e-07

def product(left_side, right_side):
    return jnp.dot(left_side.astype(jnp.float32), right_side.astype(jnp.float32), precision=lax.Precision.HIGHEST, preferred_element_type=jnp.float32)

def newton_schulz(matrix):
    frobenius = jnp.sqrt(jnp.sum(matrix * matrix))
    orthogonal = (matrix / (frobenius + NORM_EPS)).astype(jnp.bfloat16)
    for iteration in range(NS_ITERS):
        gram_matrix = product(orthogonal, orthogonal.T).astype(jnp.bfloat16)
        polynomial = (COEF_B * gram_matrix.astype(jnp.float32) + COEF_C * product(gram_matrix, gram_matrix)).astype(jnp.bfloat16)
        orthogonal = (COEF_A * orthogonal.astype(jnp.float32) + product(polynomial, orthogonal)).astype(jnp.bfloat16)
    return orthogonal

def reference(tokens, out_grads, routing, combine, weights, momentum):
    flat_expert = routing.reshape(-1).astype(jnp.int32)
    flat_weight = combine.reshape(-1)
    total = flat_expert.shape[0]
    flat_token = (jnp.arange(total, dtype=jnp.int32) // TOPK).astype(jnp.int32)
    most_rows = N_EXPERT * N_PAIR * CAP
    inv_width = 1.0 / math.sqrt(D)
    inv_hidden = 1.0 / math.sqrt(FF)
    step_size = 0.5 * math.sqrt(D)

    def per_expert(expert):
        elsewhere = (flat_expert != expert).astype(jnp.int32)
        ranking = jnp.argsort(elsewhere * total + jnp.arange(total, dtype=jnp.int32))[:most_rows].astype(jnp.int32)
        matched = elsewhere[ranking] == 0
        picked = flat_token[ranking]
        x_rows = jnp.where(matched[:, None], tokens[picked], 0).astype(jnp.bfloat16)
        scaled = out_grads[picked].astype(jnp.float32) * flat_weight[ranking][:, None]
        scaled_rows = jnp.where(matched[:, None], scaled, 0.0).astype(jnp.bfloat16)
        up_weight = weights[0, expert]
        down_weight = weights[1, expert]
        pre_act = product(x_rows, up_weight.T) * inv_width
        squash = jax.nn.sigmoid(pre_act)
        hidden = (pre_act * squash).astype(jnp.bfloat16)
        hidden_grad = product(scaled_rows, down_weight.T) * inv_hidden
        pre_grad = (hidden_grad * squash * (1.0 + pre_act * (1.0 - squash))).astype(jnp.bfloat16)
        grad_up = product(pre_grad.T, x_rows) * inv_width
        grad_down = product(hidden.T, scaled_rows) * inv_hidden
        velocity_up = DECAY * momentum[0, expert] + grad_up
        velocity_down = DECAY * momentum[1, expert] + grad_down
        new_up = (up_weight.astype(jnp.float32) - step_size * newton_schulz(velocity_up).astype(jnp.float32)).astype(jnp.bfloat16)
        new_down = (down_weight.astype(jnp.float32) - step_size * newton_schulz(velocity_down).astype(jnp.float32)).astype(jnp.bfloat16)
        return (jnp.stack([velocity_up, velocity_down]), jnp.stack([new_up, new_down]))
    velocities, updated = lax.map(per_expert, jnp.arange(EXPERTS, dtype=jnp.int32))
    return (jnp.swapaxes(velocities, 0, 1), jnp.swapaxes(updated, 0, 1))
```

```python
import math

import jax
import jax.numpy as jnp
from jax import lax
from jax.sharding import PartitionSpec as P

D = 2048
FF = 768
NS_ITERS = 2


COEF_A = 3.4445
COEF_B = -4.775
COEF_C = 2.0315
DECAY = 0.9
NORM_EPS = 1e-07
GATHER_LIMIT = 24 << 20


def contract_last(left_side, right_side):
    return lax.dot_general(
        left_side, right_side, (((1,), (1,)), ((), ())), preferred_element_type=jnp.float32
    )


def contract_first(left_side, right_side):
    return lax.dot_general(
        left_side, right_side, (((0,), (0,)), ((), ())), preferred_element_type=jnp.float32
    )


def forward_pre(x_rows, up_weight):
    return contract_last(x_rows, up_weight) * (1.0 / math.sqrt(D))


def up_gradient(x_rows, scaled_rows, pre_act, down_weight):
    squash = jax.nn.sigmoid(pre_act)
    hidden_grad = contract_last(scaled_rows, down_weight) * (1.0 / math.sqrt(FF))
    pre_grad = (hidden_grad * squash * (1.0 + pre_act * (1.0 - squash))).astype(jnp.bfloat16)
    return contract_first(pre_grad, x_rows) * (1.0 / math.sqrt(D))


def down_gradient(scaled_rows, pre_act):
    hidden = (pre_act * jax.nn.sigmoid(pre_act)).astype(jnp.bfloat16)
    return contract_first(hidden, scaled_rows) * (1.0 / math.sqrt(FF))


def newton_schulz(matrix):
    frobenius = jnp.sqrt(jnp.sum(matrix * matrix))
    orthogonal = (matrix / (frobenius + NORM_EPS)).astype(jnp.bfloat16)
    for iteration in range(NS_ITERS):
        gram_matrix = contract_last(orthogonal, orthogonal).astype(jnp.bfloat16)
        square = jnp.dot(gram_matrix, gram_matrix, preferred_element_type=jnp.float32)
        polynomial = (COEF_B * gram_matrix.astype(jnp.float32) + COEF_C * square).astype(
            jnp.bfloat16
        )
        orthogonal = (
            COEF_A * orthogonal.astype(jnp.float32)
            + jnp.dot(polynomial, orthogonal, preferred_element_type=jnp.float32)
        ).astype(jnp.bfloat16)
    return orthogonal


def sparse_rows(tokens, out_grads, routing, combine):
    tok_rows, model_width = tokens.shape
    top_count = routing.shape[1]
    n_expert = lax.axis_size("expert")
    capacity = tok_rows * top_count * 5 // (4 * n_expert) + 1
    slot_count = n_expert * capacity
    flat_expert = routing.reshape(-1)
    one_hot = (flat_expert[:, None] == jnp.arange(n_expert, dtype=jnp.int32)[None, :]).astype(
        jnp.int32
    )
    earlier = jnp.cumsum(one_hot, axis=0) - one_hot
    position = jnp.sum(earlier * one_hot, axis=1)
    target = flat_expert * capacity + position
    source = jnp.arange(flat_expert.shape[0], dtype=jnp.int32) // top_count
    slot_token = jnp.zeros((slot_count,), jnp.int32).at[target].set(source)
    slot_weight = jnp.zeros((slot_count,), jnp.float32).at[target].set(combine.reshape(-1))
    filled = jnp.zeros((slot_count,), jnp.bool_).at[target].set(True)
    x_send = jnp.where(filled[:, None], tokens[slot_token], 0).reshape(
        n_expert, capacity, model_width
    )
    scaled_send = jnp.where(
        filled[:, None], out_grads[slot_token].astype(jnp.float32) * slot_weight[:, None], 0.0
    )
    scaled_send = scaled_send.astype(jnp.bfloat16).reshape(n_expert, capacity, model_width)
    x_recv, scaled_recv = (
        lax.all_to_all(x_send, "expert", split_axis=0, concat_axis=0, tiled=True),
        lax.all_to_all(scaled_send, "expert", split_axis=0, concat_axis=0, tiled=True),
    )
    return x_recv.reshape(slot_count, model_width), scaled_recv.reshape(slot_count, model_width)


def dense_rows(tokens, out_grads, routing, combine):
    n_expert = lax.axis_size("expert")
    names = jnp.arange(n_expert, dtype=jnp.int32)[:, None, None]
    row_weight = jnp.sum(jnp.where(routing[None] == names, combine[None], 0.0), axis=2)
    row_weight = lax.all_to_all(row_weight, "expert", split_axis=0, concat_axis=0, tiled=True)
    x_rows = lax.all_gather(tokens, "expert", axis=0, tiled=True)
    grad_rows = lax.all_gather(out_grads, "expert", axis=0, tiled=True)
    scaled_rows = (grad_rows.astype(jnp.float32) * row_weight.reshape(-1, 1)).astype(jnp.bfloat16)
    return x_rows, scaled_rows


def on_device(tokens, out_grads, routing, combine, weights, momentum):
    paired = lax.all_gather(weights, "pair", axis=0, tiled=True)
    up_weight = paired[0, 0]
    down_weight = paired[1, 0]
    gathered_bytes = 2 * tokens.size * tokens.dtype.itemsize * lax.axis_size("expert")
    collect = dense_rows if gathered_bytes <= GATHER_LIMIT else sparse_rows
    x_rows, scaled_rows = collect(tokens, out_grads, routing, combine)
    pre_act = forward_pre(x_rows, up_weight)
    grad_up = up_gradient(x_rows, scaled_rows, pre_act, down_weight)
    grad_down = down_gradient(scaled_rows, pre_act)
    summed = lax.psum_scatter(
        jnp.stack([grad_up, grad_down])[:, None].astype(jnp.bfloat16),
        "pair",
        scatter_dimension=0,
        tiled=True,
    ).astype(jnp.float32)[0, 0]
    velocity = DECAY * momentum[0, 0] + summed
    orthogonal = newton_schulz(velocity)
    step_size = 0.5 * math.sqrt(D)
    updated = (
        weights[0, 0].astype(jnp.float32) - step_size * orthogonal.astype(jnp.float32)
    ).astype(jnp.bfloat16)
    rollout = lax.all_to_all(updated[None, None], "pair", split_axis=2, concat_axis=0, tiled=True)
    return (velocity[None, None], rollout)


def solution(mesh):
    return jax.shard_map(
        on_device,
        mesh=mesh,
        in_specs=(
            P(("expert", "pair"), None),
            P(("expert", "pair"), None),
            P(("expert", "pair"), None),
            P(("expert", "pair"), None),
            P("pair", "expert", None, None),
            P("pair", "expert", None, None),
        ),
        out_specs=(P("pair", "expert", None, None), P(None, "expert", "pair", None)),
        check_vma=False,
    )
```

```python
import functools
import math

import jax
import jax.numpy as jnp
from jax import lax
from jax.experimental import pallas as pl
from jax.experimental.pallas import tpu as pltpu
from jax.sharding import PartitionSpec as P

D = 2048
FF = 768
NS_ITERS = 2


COEF_A = 3.4445
COEF_B = -4.775
COEF_C = 2.0315
DECAY = 0.9
NORM_EPS = 1e-07
GATHER_LIMIT = 24 << 20
VMEM_BYTES = 60 << 20


def contract_last(left_side, right_side):
    return lax.dot_general(
        left_side, right_side, (((1,), (1,)), ((), ())), preferred_element_type=jnp.float32
    )


def contract_first(left_side, right_side):
    return lax.dot_general(
        left_side, right_side, (((0,), (0,)), ((), ())), preferred_element_type=jnp.float32
    )


def forward_pre(x_rows, up_weight):
    return contract_last(x_rows, up_weight) * (1.0 / math.sqrt(D))


def up_gradient(x_rows, scaled_rows, pre_act, down_weight):
    squash = jax.nn.sigmoid(pre_act)
    hidden_grad = contract_last(scaled_rows, down_weight) * (1.0 / math.sqrt(FF))
    pre_grad = (hidden_grad * squash * (1.0 + pre_act * (1.0 - squash))).astype(jnp.bfloat16)
    return contract_first(pre_grad, x_rows) * (1.0 / math.sqrt(D))


def down_gradient(scaled_rows, pre_act):
    hidden = (pre_act * jax.nn.sigmoid(pre_act)).astype(jnp.bfloat16)
    return contract_first(hidden, scaled_rows) * (1.0 / math.sqrt(FF))


def newton_schulz(matrix):
    frobenius = jnp.sqrt(jnp.sum(matrix * matrix))
    orthogonal = (matrix / (frobenius + NORM_EPS)).astype(jnp.bfloat16)
    for iteration in range(NS_ITERS):
        gram_matrix = contract_last(orthogonal, orthogonal).astype(jnp.bfloat16)
        square = jnp.dot(gram_matrix, gram_matrix, preferred_element_type=jnp.float32)
        polynomial = (COEF_B * gram_matrix.astype(jnp.float32) + COEF_C * square).astype(
            jnp.bfloat16
        )
        orthogonal = (
            COEF_A * orthogonal.astype(jnp.float32)
            + jnp.dot(polynomial, orthogonal, preferred_element_type=jnp.float32)
        ).astype(jnp.bfloat16)
    return orthogonal


def exchanged(tokens, out_grads, routing, combine, weights, momentum):
    tok_rows, model_width = tokens.shape
    top_count = routing.shape[1]
    n_expert = lax.axis_size("expert")
    capacity = tok_rows * top_count * 5 // (4 * n_expert) + 1
    slot_count = n_expert * capacity
    flat_expert = routing.reshape(-1)
    one_hot = (flat_expert[:, None] == jnp.arange(n_expert, dtype=jnp.int32)[None, :]).astype(
        jnp.int32
    )
    earlier = jnp.cumsum(one_hot, axis=0) - one_hot
    position = jnp.sum(earlier * one_hot, axis=1)
    target = flat_expert * capacity + position
    source = jnp.arange(flat_expert.shape[0], dtype=jnp.int32) // top_count
    slot_token = jnp.zeros((slot_count,), jnp.int32).at[target].set(source)
    slot_weight = jnp.zeros((slot_count,), jnp.float32).at[target].set(combine.reshape(-1))
    filled = jnp.zeros((slot_count,), jnp.bool_).at[target].set(True)
    x_send = jnp.where(filled[:, None], tokens[slot_token], 0).reshape(
        n_expert, capacity, model_width
    )
    scaled_send = jnp.where(
        filled[:, None], out_grads[slot_token].astype(jnp.float32) * slot_weight[:, None], 0.0
    )
    scaled_send = scaled_send.astype(jnp.bfloat16).reshape(n_expert, capacity, model_width)
    paired = lax.all_gather(weights, "pair", axis=0, tiled=True)
    up_weight = paired[0, 0]
    down_weight = paired[1, 0]
    x_recv, scaled_recv = (
        lax.all_to_all(x_send, "expert", split_axis=0, concat_axis=0, tiled=True),
        lax.all_to_all(scaled_send, "expert", split_axis=0, concat_axis=0, tiled=True),
    )
    x_rows = x_recv.reshape(slot_count, model_width)
    pre_act = forward_pre(x_rows, up_weight)
    scaled_rows = scaled_recv.reshape(slot_count, model_width)
    grad_up = up_gradient(x_rows, scaled_rows, pre_act, down_weight)
    grad_down = down_gradient(scaled_rows, pre_act)
    summed = lax.psum_scatter(
        jnp.stack([grad_up, grad_down])[:, None].astype(jnp.bfloat16),
        "pair",
        scatter_dimension=0,
        tiled=True,
    ).astype(jnp.float32)[0, 0]
    velocity = DECAY * momentum[0, 0] + summed
    orthogonal = newton_schulz(velocity)
    step_size = 0.5 * math.sqrt(D)
    updated = (
        weights[0, 0].astype(jnp.float32) - step_size * orthogonal.astype(jnp.float32)
    ).astype(jnp.bfloat16)
    rollout = lax.all_to_all(updated[None, None], "pair", split_axis=2, concat_axis=0, tiled=True)
    return (velocity[None, None], rollout)


def flipped(index, mask):
    for bit in range(mask.bit_length()):
        if (mask >> bit) & 1:
            index = index + (1 - 2 * ((index // (1 << bit)) % 2)) * (1 << bit)
    return index


def fused_kernel(
    depth, tok_hbm, grad_hbm, part_hbm, weight_hbm, momentum_hbm, velocity_hbm, rollout_hbm,
    x_buf, g_buf, c_buf, w_buf, acc, vel, out_half, in_half, scaled, hidden_t, pre_grad_t,
    ortho, gram, poly,
    x_recv, g_recv, c_recv, row_send, local_sem, pair_send, pair_recv, sum_send, sum_recv,
    roll_send, roll_recv, roll_local,
):
    rows, width = tok_hbm.shape
    hidden_units = w_buf.shape[1]
    me = lax.axis_index("expert")
    pair = lax.axis_index("pair")
    beside = {"expert": me + 1 - 2 * (me % 2)}
    across = {"expert": flipped(me, 2)}
    partner = {"pair": 1 - pair}
    above = [{"expert": flipped(me // 4, d) * 4 + me % 4} for d in range(1, depth)]
    mesh_id = pl.DeviceIdType.MESH

    arrivals = ((x_buf, x_recv), (g_buf, g_recv), (c_buf, c_recv))
    sent = []

    def send(which, slot, to_slot, device):
        buf, recv = arrivals[which]
        copy = pltpu.make_async_remote_copy(
            buf.at[slot], buf.at[to_slot], row_send.at[len(sent)], recv.at[to_slot],
            device_id=device, device_id_type=mesh_id,
        )
        copy.start()
        sent.append(copy)

    def arrive(slot, which):
        buf, recv = arrivals[which]
        pltpu.make_async_remote_copy(
            buf.at[slot], buf.at[slot], row_send.at[0], recv.at[slot],
            device_id=beside, device_id_type=mesh_id,
        ).wait_recv()

    loads = [
        pltpu.make_async_copy(source, target, local_sem.at[i])
        for i, (source, target) in enumerate((
            (tok_hbm, x_buf.at[0]), (grad_hbm, g_buf.at[0]), (part_hbm, c_buf.at[0]),
            (weight_hbm.at[0, 0], w_buf.at[pair]), (momentum_hbm.at[0, 0], vel),
        ))
    ]
    for load in loads:
        load.start()
    barrier = pltpu.get_barrier_semaphore()
    near = above + [beside, across, partner]
    for device in near:
        pl.semaphore_signal(barrier, inc=1, device_id=device, device_id_type=mesh_id)
    pl.semaphore_wait(barrier, len(near))
    for load in loads[:3]:
        load.wait()

    for which in range(3):
        send(which, 0, depth, beside)
        send(which, 0, 2 * depth, across)
        send(which, 0, 1, above[0])
    for d in range(2, depth):
        for which in range(3):
            send(which, 0, d, above[d - 1])
    loads[3].wait()
    weight_copy = pltpu.make_async_remote_copy(
        w_buf.at[pair], w_buf.at[pair], pair_send.at[0], pair_recv.at[0],
        device_id=partner, device_id_type=mesh_id,
    )
    weight_copy.start()

    tile = 256
    n_hidden = hidden_units // tile
    n_width = width // tile

    def clear(i, carry):
        part = pl.ds(pl.multiple_of(i * 128, 128), 128)
        for m in range(2):
            acc[m, part, :] = jnp.zeros((128, width), jnp.float32)
        return carry

    lax.fori_loop(0, hidden_units // 128, clear, 0)
    for d in range(1, depth):
        for which in range(3):
            arrive(d, which)
            send(which, d, depth + d, beside)
            send(which, d, 2 * depth + d, across)
    pltpu.make_async_remote_copy(
        w_buf.at[pair], w_buf.at[1 - pair], pair_send.at[0], pair_recv.at[0],
        device_id=partner, device_id_type=mesh_id,
    ).wait_recv()

    diagonal = lax.broadcasted_iota(jnp.int32, (rows, rows), 0) == lax.broadcasted_iota(
        jnp.int32, (rows, rows), 1
    )

    def gradients(slot):
        for i in range(2):
            line = c_buf[slot + i, pl.ds(me, 1), :]
            column = jnp.sum(jnp.where(diagonal, line, 0.0), axis=1, keepdims=True)

            def scale(j, carry, i=i, column=column):
                cols = pl.ds(pl.multiple_of(j * tile, tile), tile)
                scaled[i * rows:(i + 1) * rows, cols] = (
                    g_buf[slot + i, :, cols].astype(jnp.float32) * column
                ).astype(jnp.bfloat16)
                return carry

            lax.fori_loop(0, n_width, scale, 0)

        def activate(i, carry):
            part = pl.ds(pl.multiple_of(i * tile, tile), tile)
            x_rows = x_buf[pl.ds(slot, 2)].reshape(2 * rows, width)
            pre = contract_last(x_rows, w_buf[0, part, :]) * (1.0 / math.sqrt(width))
            hidden_grad = contract_last(scaled[...], w_buf[1, part, :]) * (
                1.0 / math.sqrt(hidden_units)
            )
            squash = jax.nn.sigmoid(pre)
            hidden_t[part, :] = (pre * squash).T.astype(jnp.bfloat16)
            pre_grad_t[part, :] = (
                hidden_grad * squash * (1.0 + pre * (1.0 - squash))
            ).T.astype(jnp.bfloat16)
            return carry

        lax.fori_loop(0, n_hidden, activate, 0)

        def outer(j, carry):
            cols = pl.ds(pl.multiple_of(j * tile, tile), tile)
            x_cols = x_buf[pl.ds(slot, 2), :, cols].reshape(2 * rows, tile)
            acc[0, :, cols] += jnp.dot(
                pre_grad_t[...], x_cols, preferred_element_type=jnp.float32
            )
            acc[1, :, cols] += jnp.dot(
                hidden_t[...], scaled[:, cols], preferred_element_type=jnp.float32
            )
            return carry

        lax.fori_loop(0, n_width, outer, 0)

    def several(first, stride, count):
        def one(i, carry):
            gradients(first + i * stride)
            return carry

        lax.fori_loop(0, count, one, 0)

    several(0, 2, depth // 2)
    for d in range(0, depth, 2):
        for k in (d, d + 1):
            arrive(depth + k, 1)
            send(1, depth + k, 3 * depth + k, across)
            arrive(2 * depth + k, 0)
            send(0, 2 * depth + k, 3 * depth + k, beside)
            arrive(2 * depth + k, 2)
            send(2, 2 * depth + k, 3 * depth + k, beside)
        for k in (d, d + 1):
            arrive(depth + k, 0)
            arrive(depth + k, 2)
            arrive(2 * depth + k, 1)
        several(depth + d, depth, 2)
    for d in range(0, depth, 2):
        for k in (d, d + 1):
            for which in range(3):
                arrive(3 * depth + k, which)
        gradients(3 * depth + d)

    inv_width, inv_hidden = 1.0 / math.sqrt(width), 1.0 / math.sqrt(hidden_units)
    own_scale = jnp.where(pair == 0, inv_width, inv_hidden).astype(jnp.float32)
    other_scale = jnp.where(pair == 0, inv_hidden, inv_width).astype(jnp.float32)

    def sum_copy(t):
        part = pl.ds(pl.multiple_of(t * 128, 128), 128)
        return pltpu.make_async_remote_copy(
            out_half.at[part], in_half.at[part], sum_send.at[t], sum_recv.at[t],
            device_id=partner, device_id_type=mesh_id,
        )

    def give(t, carry):
        part = pl.ds(pl.multiple_of(t * 128, 128), 128)
        out_half[part, :] = (acc[1 - pair, part, :] * other_scale).astype(jnp.bfloat16)
        sum_copy(t).start()
        return carry

    steps = hidden_units // 128
    lax.fori_loop(0, steps, give, 0)
    loads[4].wait()

    def take(t, squares):
        part = pl.ds(pl.multiple_of(t * 128, 128), 128)
        sum_copy(t).wait_recv()
        new = DECAY * vel[part, :] + (
            acc[pair, part, :] * own_scale + in_half[part, :].astype(jnp.float32)
        )
        vel[part, :] = new
        return squares + jnp.sum(new * new, axis=0, keepdims=True)

    squares = lax.fori_loop(0, steps, take, jnp.zeros((1, width), jnp.float32))
    store = pltpu.make_async_copy(vel, velocity_hbm.at[0, 0], local_sem.at[5])
    store.start()
    inverse = 1.0 / (jnp.sqrt(jnp.sum(squares, axis=1, keepdims=True)) + NORM_EPS)

    def normalise(t, carry):
        part = pl.ds(pl.multiple_of(t * 128, 128), 128)
        ortho[part, :] = (vel[part, :] * inverse).astype(jnp.bfloat16)
        sum_copy(t).wait_send()
        return carry

    lax.fori_loop(0, steps, normalise, 0)

    half = hidden_units // 2
    step_size = 0.5 * math.sqrt(width)

    def roll_copies(j):
        cols = pl.ds(pl.multiple_of(j * tile, tile), tile)
        away = pltpu.make_async_remote_copy(
            out_half.at[pl.ds(pl.multiple_of((1 - pair) * half, 128), half), cols],
            rollout_hbm.at[pair, 0, :, cols], roll_send.at[j], roll_recv.at[j],
            device_id=partner, device_id_type=mesh_id,
        )
        back = pltpu.make_async_remote_copy(
            out_half.at[pl.ds(pl.multiple_of((1 - pair) * half, 128), half), cols],
            rollout_hbm.at[1 - pair, 0, :, cols], roll_send.at[j], roll_recv.at[j],
            device_id=partner, device_id_type=mesh_id,
        )
        stay = pltpu.make_async_copy(
            out_half.at[pl.ds(pl.multiple_of(pair * half, 128), half), cols],
            rollout_hbm.at[pair, 0, :, cols], roll_local.at[j],
        )
        return away, back, stay

    for iteration in range(NS_ITERS):
        def gram_rows(i, carry):
            part = pl.ds(pl.multiple_of(i * tile, tile), tile)
            gram[part, :] = contract_last(ortho[part, :], ortho[...]).astype(jnp.bfloat16)
            return carry

        lax.fori_loop(0, n_hidden, gram_rows, 0)

        def poly_rows(i, carry):
            part = pl.ds(pl.multiple_of(i * tile, tile), tile)
            square = jnp.dot(gram[part, :], gram[...], preferred_element_type=jnp.float32)
            poly[part, :] = (COEF_B * gram[part, :].astype(jnp.float32) + COEF_C * square).astype(
                jnp.bfloat16
            )
            return carry

        lax.fori_loop(0, n_hidden, poly_rows, 0)

        def advance(j, carry, last=iteration == NS_ITERS - 1):
            cols = pl.ds(pl.multiple_of(j * tile, tile), tile)
            old = ortho[:, cols]
            new = (
                COEF_A * old.astype(jnp.float32)
                + jnp.dot(poly[...], old, preferred_element_type=jnp.float32)
            ).astype(jnp.bfloat16)
            if last:
                out_half[:, cols] = (
                    w_buf[pair, :, cols].astype(jnp.float32) - step_size * new.astype(jnp.float32)
                ).astype(jnp.bfloat16)
                away, _, stay = roll_copies(j)
                away.start()
                stay.start()
            else:
                ortho[:, cols] = new
            return carry

        lax.fori_loop(0, n_width, advance, 0)

    for copy in sent:
        copy.wait_send()
    weight_copy.wait_send()

    def finish(j, carry):
        away, back, stay = roll_copies(j)
        away.wait_send()
        back.wait_recv()
        stay.wait()
        return carry

    lax.fori_loop(0, n_width, finish, 0)
    store.wait()


def fused(tokens, out_grads, routing, combine, weights, momentum):
    n_expert = lax.axis_size("expert")
    depth = n_expert // 4
    rows, width = tokens.shape
    hidden_units = weights.shape[2]
    slots = 4 * depth
    names = jnp.arange(n_expert, dtype=jnp.int32)[:, None, None]
    row_weight = jnp.sum(jnp.where(routing[None] == names, combine[None], 0.0), axis=2)
    half_shape = (2, 1, hidden_units // 2, width)
    any_space = pl.BlockSpec(memory_space=pl.ANY)
    matrix = (hidden_units, width)
    sends = 3 * (depth - 1) + 9 * depth
    dma = pltpu.SemaphoreType.DMA
    return pl.pallas_call(
        functools.partial(fused_kernel, depth),
        out_shape=(
            jax.ShapeDtypeStruct(momentum.shape, jnp.float32),
            jax.ShapeDtypeStruct(half_shape, jnp.bfloat16),
        ),
        in_specs=[any_space] * 5,
        out_specs=(any_space, any_space),
        scratch_shapes=[
            pltpu.VMEM((slots, rows, width), jnp.bfloat16),
            pltpu.VMEM((slots, rows, width), jnp.bfloat16),
            pltpu.VMEM((slots, n_expert, rows), jnp.float32),
            pltpu.VMEM((2,) + matrix, jnp.bfloat16),
            pltpu.VMEM((2,) + matrix, jnp.float32),
            pltpu.VMEM(matrix, jnp.float32),
            pltpu.VMEM(matrix, jnp.bfloat16),
            pltpu.VMEM(matrix, jnp.bfloat16),
            pltpu.VMEM((2 * rows, width), jnp.bfloat16),
            pltpu.VMEM((hidden_units, 2 * rows), jnp.bfloat16),
            pltpu.VMEM((hidden_units, 2 * rows), jnp.bfloat16),
            pltpu.VMEM(matrix, jnp.bfloat16),
            pltpu.VMEM((hidden_units, hidden_units), jnp.bfloat16),
            pltpu.VMEM((hidden_units, hidden_units), jnp.bfloat16),
            dma((slots,)),
            dma((slots,)),
            dma((slots,)),
            dma((sends,)),
            dma((6,)),
            dma((1,)),
            dma((1,)),
            dma((hidden_units // 128,)),
            dma((hidden_units // 128,)),
            dma((width // 256,)),
            dma((width // 256,)),
            dma((width // 256,)),
        ],
        compiler_params=pltpu.CompilerParams(
            collective_id=0, has_side_effects=True, vmem_limit_bytes=VMEM_BYTES
        ),
    )(tokens, out_grads, row_weight, weights, momentum)


def on_device(tokens, out_grads, routing, combine, weights, momentum):
    gathered_bytes = 2 * tokens.size * tokens.dtype.itemsize * lax.axis_size("expert")
    step = fused if gathered_bytes <= GATHER_LIMIT else exchanged
    return step(tokens, out_grads, routing, combine, weights, momentum)


def solution(mesh):
    return jax.shard_map(
        on_device,
        mesh=mesh,
        in_specs=(
            P(("expert", "pair"), None),
            P(("expert", "pair"), None),
            P(("expert", "pair"), None),
            P(("expert", "pair"), None),
            P("pair", "expert", None, None),
            P("pair", "expert", None, None),
        ),
        out_specs=(P("pair", "expert", None, None), P(None, "expert", "pair", None)),
        check_vma=False,
    )
```

```python
import functools
import math

import jax
import jax.numpy as jnp
from jax import lax
from jax.experimental import pallas as pl
from jax.experimental.pallas import tpu as pltpu
from jax.sharding import PartitionSpec as P

D = 2048
FF = 768
NS_ITERS = 2


COEF_A = 3.4445
COEF_B = -4.775
COEF_C = 2.0315
DECAY = 0.9
NORM_EPS = 1e-07
GATHER_LIMIT = 24 << 20
VMEM_BYTES = 60 << 20


def contract_last(left_side, right_side):
    return lax.dot_general(
        left_side, right_side, (((1,), (1,)), ((), ())), preferred_element_type=jnp.float32
    )


def contract_first(left_side, right_side):
    return lax.dot_general(
        left_side, right_side, (((0,), (0,)), ((), ())), preferred_element_type=jnp.float32
    )


def forward_pre(x_rows, up_weight):
    return contract_last(x_rows, up_weight) * (1.0 / math.sqrt(D))


def up_gradient(x_rows, scaled_rows, pre_act, down_weight):
    squash = jax.nn.sigmoid(pre_act)
    hidden_grad = contract_last(scaled_rows, down_weight) * (1.0 / math.sqrt(FF))
    pre_grad = (hidden_grad * squash * (1.0 + pre_act * (1.0 - squash))).astype(jnp.bfloat16)
    return contract_first(pre_grad, x_rows) * (1.0 / math.sqrt(D))


def down_gradient(scaled_rows, pre_act):
    hidden = (pre_act * jax.nn.sigmoid(pre_act)).astype(jnp.bfloat16)
    return contract_first(hidden, scaled_rows) * (1.0 / math.sqrt(FF))


def newton_schulz(matrix):
    frobenius = jnp.sqrt(jnp.sum(matrix * matrix))
    orthogonal = (matrix / (frobenius + NORM_EPS)).astype(jnp.bfloat16)
    for iteration in range(NS_ITERS):
        gram_matrix = contract_last(orthogonal, orthogonal).astype(jnp.bfloat16)
        square = jnp.dot(gram_matrix, gram_matrix, preferred_element_type=jnp.float32)
        polynomial = (COEF_B * gram_matrix.astype(jnp.float32) + COEF_C * square).astype(
            jnp.bfloat16
        )
        orthogonal = (
            COEF_A * orthogonal.astype(jnp.float32)
            + jnp.dot(polynomial, orthogonal, preferred_element_type=jnp.float32)
        ).astype(jnp.bfloat16)
    return orthogonal


def exchanged(tokens, out_grads, routing, combine, weights, momentum):
    tok_rows, model_width = tokens.shape
    top_count = routing.shape[1]
    n_expert = lax.axis_size("expert")
    capacity = tok_rows * top_count * 5 // (4 * n_expert) + 1
    slot_count = n_expert * capacity
    flat_expert = routing.reshape(-1)
    one_hot = (flat_expert[:, None] == jnp.arange(n_expert, dtype=jnp.int32)[None, :]).astype(
        jnp.int32
    )
    earlier = jnp.cumsum(one_hot, axis=0) - one_hot
    position = jnp.sum(earlier * one_hot, axis=1)
    target = flat_expert * capacity + position
    source = jnp.arange(flat_expert.shape[0], dtype=jnp.int32) // top_count
    slot_token = jnp.zeros((slot_count,), jnp.int32).at[target].set(source)
    slot_weight = jnp.zeros((slot_count,), jnp.float32).at[target].set(combine.reshape(-1))
    filled = jnp.zeros((slot_count,), jnp.bool_).at[target].set(True)
    x_send = jnp.where(filled[:, None], tokens[slot_token], 0).reshape(
        n_expert, capacity, model_width
    )
    scaled_send = jnp.where(
        filled[:, None], out_grads[slot_token].astype(jnp.float32) * slot_weight[:, None], 0.0
    )
    scaled_send = scaled_send.astype(jnp.bfloat16).reshape(n_expert, capacity, model_width)
    paired = lax.all_gather(weights, "pair", axis=0, tiled=True)
    up_weight = paired[0, 0]
    down_weight = paired[1, 0]
    x_recv, scaled_recv = (
        lax.all_to_all(x_send, "expert", split_axis=0, concat_axis=0, tiled=True),
        lax.all_to_all(scaled_send, "expert", split_axis=0, concat_axis=0, tiled=True),
    )
    x_rows = x_recv.reshape(slot_count, model_width)
    pre_act = forward_pre(x_rows, up_weight)
    scaled_rows = scaled_recv.reshape(slot_count, model_width)
    grad_up = up_gradient(x_rows, scaled_rows, pre_act, down_weight)
    grad_down = down_gradient(scaled_rows, pre_act)
    summed = lax.psum_scatter(
        jnp.stack([grad_up, grad_down])[:, None].astype(jnp.bfloat16),
        "pair",
        scatter_dimension=0,
        tiled=True,
    ).astype(jnp.float32)[0, 0]
    velocity = DECAY * momentum[0, 0] + summed
    orthogonal = newton_schulz(velocity)
    step_size = 0.5 * math.sqrt(D)
    updated = (
        weights[0, 0].astype(jnp.float32) - step_size * orthogonal.astype(jnp.float32)
    ).astype(jnp.bfloat16)
    rollout = lax.all_to_all(updated[None, None], "pair", split_axis=2, concat_axis=0, tiled=True)
    return (velocity[None, None], rollout)


def flipped(index, mask):
    for bit in range(mask.bit_length()):
        if (mask >> bit) & 1:
            index = index + (1 - 2 * ((index // (1 << bit)) % 2)) * (1 << bit)
    return index


def fused_kernel(
    depth, tok_hbm, grad_hbm, part_hbm, weight_hbm, momentum_hbm, velocity_hbm, rollout_hbm,
    x_buf, g_buf, c_buf, w_buf, acc, vel, out_half, in_half, row_pair, slope,
    ortho, gram, poly,
    x_recv, g_recv, c_recv, row_send, local_sem, pair_send, pair_recv, sum_send, sum_recv,
    roll_send, roll_recv, roll_local,
):
    rows, width = tok_hbm.shape
    hidden_units = w_buf.shape[1]
    me = lax.axis_index("expert")
    pair = lax.axis_index("pair")
    beside = {"expert": me + 1 - 2 * (me % 2)}
    across = {"expert": flipped(me, 2)}
    partner = {"pair": 1 - pair}
    above = [{"expert": flipped(me // 4, d) * 4 + me % 4} for d in range(1, depth)]
    mesh_id = pl.DeviceIdType.MESH

    arrivals = ((x_buf, x_recv), (g_buf, g_recv), (c_buf, c_recv))
    sent = []

    def piece(which, slot, upper):
        ref = arrivals[which][0].at[slot]
        return ref if upper is None else ref.at[pl.ds(upper * (rows // 2), rows // 2)]

    def send(which, slot, to_slot, device, upper=None):
        copy = pltpu.make_async_remote_copy(
            piece(which, slot, upper), piece(which, to_slot, upper), row_send.at[len(sent)],
            arrivals[which][1].at[to_slot + (upper or 0)],
            device_id=device, device_id_type=mesh_id,
        )
        copy.start()
        sent.append(copy)

    def arrive(slot, which, upper=None):
        part = piece(which, slot, upper)
        pltpu.make_async_remote_copy(
            part, part, row_send.at[0], arrivals[which][1].at[slot + (upper or 0)],
            device_id=beside, device_id_type=mesh_id,
        ).wait_recv()

    loads = [
        pltpu.make_async_copy(source, target, local_sem.at[i])
        for i, (source, target) in enumerate((
            (tok_hbm, x_buf.at[0]), (grad_hbm, g_buf.at[0]), (part_hbm, c_buf.at[0]),
            (weight_hbm.at[0, 0], w_buf.at[pair]), (momentum_hbm.at[0, 0], vel),
        ))
    ]
    for load in loads:
        load.start()
    barrier = pltpu.get_barrier_semaphore()
    near = above + [beside, across, partner]
    for device in near:
        pl.semaphore_signal(barrier, inc=1, device_id=device, device_id_type=mesh_id)
    pl.semaphore_wait(barrier, len(near))
    for load in loads[:3]:
        load.wait()

    for which in range(3):
        send(which, 0, depth, beside)
        send(which, 0, 2 * depth, across)
        send(which, 0, 1, above[0])
    for d in range(2, depth):
        for which in range(3):
            send(which, 0, d, above[d - 1])
    loads[3].wait()
    weight_copy = pltpu.make_async_remote_copy(
        w_buf.at[pair], w_buf.at[pair], pair_send.at[0], pair_recv.at[0],
        device_id=partner, device_id_type=mesh_id,
    )
    weight_copy.start()

    tile = 256
    n_hidden = hidden_units // tile
    n_width = width // tile

    def clear(i, carry):
        part = pl.ds(pl.multiple_of(i * 128, 128), 128)
        for m in range(2):
            acc[m, part, :] = jnp.zeros((128, width), jnp.float32)
        return carry

    def relay(k, upper=None):
        arrive(depth + k, 1)
        send(1, depth + k, 3 * depth + k, across, upper)
        arrive(2 * depth + k, 0)
        send(0, 2 * depth + k, 3 * depth + k, beside, upper)
        arrive(2 * depth + k, 2)
        send(2, 2 * depth + k, 3 * depth + k, beside)

    def rest(k):
        arrive(depth + k, 0)
        arrive(depth + k, 2)
        arrive(2 * depth + k, 1)

    def column(d):
        for which in range(3):
            arrive(d, which)
            send(which, d, depth + d, beside)
            send(which, d, 2 * depth + d, across)

    lax.fori_loop(0, hidden_units // 128, clear, 0)
    relay(0)
    column(1)
    pltpu.make_async_remote_copy(
        w_buf.at[pair], w_buf.at[1 - pair], pair_send.at[0], pair_recv.at[0],
        device_id=partner, device_id_type=mesh_id,
    ).wait_recv()

    diagonal = lax.broadcasted_iota(jnp.int32, (rows, rows), 0) == lax.broadcasted_iota(
        jnp.int32, (rows, rows), 1
    )

    def activations(slot):
        for i in range(2):
            line = c_buf[slot + i, pl.ds(me, 1), :]
            column = jnp.sum(jnp.where(diagonal, line, 0.0), axis=1, keepdims=True)

            def scale(j, carry, i=i, column=column):
                cols = pl.ds(pl.multiple_of(j * tile, tile), tile)
                row_pair[1, i * rows:(i + 1) * rows, cols] = (
                    g_buf[slot + i, :, cols].astype(jnp.float32) * column
                ).astype(jnp.bfloat16)
                return carry

            lax.fori_loop(0, n_width, scale, 0)

        def activate(i, carry):
            part = pl.ds(pl.multiple_of(i * tile, tile), tile)
            x_rows = x_buf[pl.ds(slot, 2)].reshape(2 * rows, width)
            pre = contract_last(x_rows, w_buf[0, part, :]) * (1.0 / math.sqrt(width))
            hidden_grad = contract_last(row_pair[1], w_buf[1, part, :]) * (
                1.0 / math.sqrt(hidden_units)
            )
            squash = jax.nn.sigmoid(pre)
            slope[1, part, :] = (pre * squash).T.astype(jnp.bfloat16)
            slope[0, part, :] = (
                hidden_grad * squash * (1.0 + pre * (1.0 - squash))
            ).T.astype(jnp.bfloat16)
            return carry

        lax.fori_loop(0, n_hidden, activate, 0)

    def gradients(slot):
        activations(slot)

        def outer(j, carry):
            cols = pl.ds(pl.multiple_of(j * tile, tile), tile)
            x_cols = x_buf[pl.ds(slot, 2), :, cols].reshape(2 * rows, tile)
            acc[0, :, cols] += jnp.dot(
                slope[0], x_cols, preferred_element_type=jnp.float32
            )
            acc[1, :, cols] += jnp.dot(
                slope[1], row_pair[1, :, cols], preferred_element_type=jnp.float32
            )
            return carry

        lax.fori_loop(0, n_width, outer, 0)

    def several(first, stride, count):
        def one(i, carry):
            gradients(first + i * stride)
            return carry

        lax.fori_loop(0, count, one, 0)

    last = depth - 1
    gradients(0)
    for d in range(2, depth, 2):
        column(d)
        if d == 2:
            for which in range(3):
                arrive(3 * depth, which)
                send(which, 3 * depth, 3 * depth + 1, above[0])
            for which in range(2):
                send(which, 3 * depth, 3 * depth + last, above[last - 1], 0)
            for which in range(3):
                arrive(depth + 1, which)
                arrive(2 * depth + 1, which)
            rest(0)
            several(depth, depth, 2)
        column(d + 1)
        gradients(d)
        relay(d)
        relay(d + 1, 1 if d + 1 == last else None)
        rest(d)
        rest(d + 1)
        several(depth + d, depth, 2)
    for d in range(0, depth, 2):
        for k in (d, d + 1):
            for which in range(3):
                if which < 2 and k == last:
                    arrive(3 * depth + k, which, 0)
                    arrive(3 * depth + k, which, 1)
                elif k > 0:
                    arrive(3 * depth + k, which)
        if d + 2 < depth:
            gradients(3 * depth + d)
    final = 4 * depth - 2
    activations(final)
    row_pair[0] = x_buf[final:final + 2].reshape(2 * rows, width)

    inv_width, inv_hidden = 1.0 / math.sqrt(width), 1.0 / math.sqrt(hidden_units)
    own_scale = jnp.where(pair == 0, inv_width, inv_hidden).astype(jnp.float32)
    other_scale = jnp.where(pair == 0, inv_hidden, inv_width).astype(jnp.float32)

    def sum_copy(j):
        cols = pl.ds(pl.multiple_of(j * tile, tile), tile)
        return pltpu.make_async_remote_copy(
            out_half.at[:, cols], in_half.at[:, cols], sum_send.at[j], sum_recv.at[j],
            device_id=partner, device_id_type=mesh_id,
        )

    def total(m, cols):
        return acc[m, :, cols] + jnp.dot(
            slope[m], row_pair[m, :, cols], preferred_element_type=jnp.float32
        )

    def give(j, carry):
        cols = pl.ds(pl.multiple_of(j * tile, tile), tile)
        out_half[:, cols] = (total(1 - pair, cols) * other_scale).astype(jnp.bfloat16)
        sum_copy(j).start()
        return carry

    lax.fori_loop(0, n_width, give, 0)
    loads[4].wait()

    def take(j, squares):
        cols = pl.ds(pl.multiple_of(j * tile, tile), tile)
        own = DECAY * vel[:, cols] + total(pair, cols) * own_scale
        sum_copy(j).wait_recv()
        new = own + in_half[:, cols].astype(jnp.float32)
        vel[:, cols] = new
        return squares + jnp.sum(new * new, axis=0, keepdims=True)

    squares = lax.fori_loop(0, n_width, take, jnp.zeros((1, tile), jnp.float32))
    store = pltpu.make_async_copy(vel, velocity_hbm.at[0, 0], local_sem.at[5])
    store.start()
    inverse = 1.0 / (jnp.sqrt(jnp.sum(squares, axis=1, keepdims=True)) + NORM_EPS)

    def normalise(t, carry):
        part = pl.ds(pl.multiple_of(t * 128, 128), 128)
        ortho[part, :] = (vel[part, :] * inverse).astype(jnp.bfloat16)
        return carry

    lax.fori_loop(0, hidden_units // 128, normalise, 0)

    def sum_sent(j, carry):
        sum_copy(j).wait_send()
        return carry

    lax.fori_loop(0, n_width, sum_sent, 0)

    half = hidden_units // 2
    step_size = 0.5 * math.sqrt(width)

    def roll_copies(j):
        cols = pl.ds(pl.multiple_of(j * tile, tile), tile)
        away = pltpu.make_async_remote_copy(
            out_half.at[pl.ds(pl.multiple_of((1 - pair) * half, 128), half), cols],
            rollout_hbm.at[pair, 0, :, cols], roll_send.at[j], roll_recv.at[j],
            device_id=partner, device_id_type=mesh_id,
        )
        back = pltpu.make_async_remote_copy(
            out_half.at[pl.ds(pl.multiple_of((1 - pair) * half, 128), half), cols],
            rollout_hbm.at[1 - pair, 0, :, cols], roll_send.at[j], roll_recv.at[j],
            device_id=partner, device_id_type=mesh_id,
        )
        stay = pltpu.make_async_copy(
            out_half.at[pl.ds(pl.multiple_of(pair * half, 128), half), cols],
            rollout_hbm.at[pair, 0, :, cols], roll_local.at[j],
        )
        return away, back, stay

    for iteration in range(NS_ITERS):
        def gram_rows(i, carry):
            part = pl.ds(pl.multiple_of(i * tile, tile), tile)
            gram[part, :] = contract_last(ortho[part, :], ortho[...]).astype(jnp.bfloat16)
            return carry

        lax.fori_loop(0, n_hidden, gram_rows, 0)

        def poly_rows(i, carry):
            part = pl.ds(pl.multiple_of(i * tile, tile), tile)
            square = jnp.dot(gram[part, :], gram[...], preferred_element_type=jnp.float32)
            poly[part, :] = (COEF_B * gram[part, :].astype(jnp.float32) + COEF_C * square).astype(
                jnp.bfloat16
            )
            return carry

        lax.fori_loop(0, n_hidden, poly_rows, 0)

        def advance(j, carry, last=iteration == NS_ITERS - 1):
            cols = pl.ds(pl.multiple_of(j * tile, tile), tile)
            old = ortho[:, cols]
            new = (
                COEF_A * old.astype(jnp.float32)
                + jnp.dot(poly[...], old, preferred_element_type=jnp.float32)
            ).astype(jnp.bfloat16)
            if last:
                out_half[:, cols] = (
                    w_buf[pair, :, cols].astype(jnp.float32) - step_size * new.astype(jnp.float32)
                ).astype(jnp.bfloat16)
                away, _, stay = roll_copies(j)
                away.start()
                stay.start()
            else:
                ortho[:, cols] = new
            return carry

        lax.fori_loop(0, n_width, advance, 0)

    for copy in sent:
        copy.wait_send()
    weight_copy.wait_send()

    def finish(j, carry):
        away, back, stay = roll_copies(j)
        away.wait_send()
        back.wait_recv()
        stay.wait()
        return carry

    lax.fori_loop(0, n_width, finish, 0)
    store.wait()


def fused(tokens, out_grads, routing, combine, weights, momentum):
    n_expert = lax.axis_size("expert")
    depth = n_expert // 4
    rows, width = tokens.shape
    hidden_units = weights.shape[2]
    slots = 4 * depth
    names = jnp.arange(n_expert, dtype=jnp.int32)[:, None, None]
    row_weight = jnp.sum(jnp.where(routing[None] == names, combine[None], 0.0), axis=2)
    half_shape = (2, 1, hidden_units // 2, width)
    any_space = pl.BlockSpec(memory_space=pl.ANY)
    matrix = (hidden_units, width)
    sends = 3 * (depth - 1) + 9 * depth + 2
    dma = pltpu.SemaphoreType.DMA
    return pl.pallas_call(
        functools.partial(fused_kernel, depth),
        out_shape=(
            jax.ShapeDtypeStruct(momentum.shape, jnp.float32),
            jax.ShapeDtypeStruct(half_shape, jnp.bfloat16),
        ),
        in_specs=[any_space] * 5,
        out_specs=(any_space, any_space),
        scratch_shapes=[
            pltpu.VMEM((slots, rows, width), jnp.bfloat16),
            pltpu.VMEM((slots, rows, width), jnp.bfloat16),
            pltpu.VMEM((slots, n_expert, rows), jnp.float32),
            pltpu.VMEM((2,) + matrix, jnp.bfloat16),
            pltpu.VMEM((2,) + matrix, jnp.float32),
            pltpu.VMEM(matrix, jnp.float32),
            pltpu.VMEM(matrix, jnp.bfloat16),
            pltpu.VMEM(matrix, jnp.bfloat16),
            pltpu.VMEM((2, 2 * rows, width), jnp.bfloat16),
            pltpu.VMEM((2, hidden_units, 2 * rows), jnp.bfloat16),
            pltpu.VMEM(matrix, jnp.bfloat16),
            pltpu.VMEM((hidden_units, hidden_units), jnp.bfloat16),
            pltpu.VMEM((hidden_units, hidden_units), jnp.bfloat16),
            dma((slots + 1,)),
            dma((slots + 1,)),
            dma((slots,)),
            dma((sends,)),
            dma((6,)),
            dma((1,)),
            dma((1,)),
            dma((width // 256,)),
            dma((width // 256,)),
            dma((width // 256,)),
            dma((width // 256,)),
            dma((width // 256,)),
        ],
        compiler_params=pltpu.CompilerParams(
            collective_id=0, has_side_effects=True, vmem_limit_bytes=VMEM_BYTES
        ),
    )(tokens, out_grads, row_weight, weights, momentum)


def on_device(tokens, out_grads, routing, combine, weights, momentum):
    gathered_bytes = 2 * tokens.size * tokens.dtype.itemsize * lax.axis_size("expert")
    step = fused if gathered_bytes <= GATHER_LIMIT else exchanged
    return step(tokens, out_grads, routing, combine, weights, momentum)


def solution(mesh):
    return jax.shard_map(
        on_device,
        mesh=mesh,
        in_specs=(
            P(("expert", "pair"), None),
            P(("expert", "pair"), None),
            P(("expert", "pair"), None),
            P(("expert", "pair"), None),
            P("pair", "expert", None, None),
            P("pair", "expert", None, None),
        ),
        out_specs=(P("pair", "expert", None, None), P(None, "expert", "pair", None)),
        check_vma=False,
    )
```
